256 devices in a mesh: snap: 64 (over x, y_lo, z), bin: 4 (over y_hi, core).
Axes of the slice: x: 4, y: 4 (y_hi: 2, y_lo: 2; y = y_hi * 2 + y_lo), z: 8, core: 2. Of those that a mesh axis runs over, the one named last changes fastest.
Arguments:
- data: bfloat16 [256, 1024, 1024], P(None, ('snap', 'bin')), may hold values from -6 to 6
- steering: bfloat16 [256, 1024, 2048], P(('snap', 'bin')), may hold values from -2 to 2
- start: float32 [256, 1024, 64], P(('snap', 'bin')), may hold values from -6 to 6
Outputs:
- projector: float32 [256, 1024, 1024], P(('snap', 'bin'))
- spectrum: float32 [2048], replicated
The draws below stay inside these ranges and needn't reach their ends.
All inputs are finite; a program needn't handle non-finite values.
Results may differ from the reference program's by a relative error of at most 0.00042.
Values may be sent and summed in bfloat16 or wider, within the bound.
No kernel may reach another device: no remote copies, remote signals or barrier semaphores. Data moves between devices by JAX's collectives and lax.ppermute only.
A program may use at most 64 MiB of HBM per device.

```python
import math
import jax
import jax.numpy as jnp
from jax import lax

M = 1024
F = 256
SOURCES = 64
G = 2048
ITERS = 3
K2 = 1024


def array_pieces(key):
    sines = jax.random.uniform(jax.random.fold_in(key, 101), (G,), jnp.float32, -1.0, 1.0)
    fraction = jax.random.uniform(jax.random.fold_in(key, 102), (F,), jnp.float32, 0.5, 1.0)
    gains = jnp.exp(jax.random.uniform(jax.random.fold_in(key, 103), (F, M), jnp.float32, -0.34, 0.34))
    return (sines, fraction, gains)


def steer_columns(fraction, gains, sines):
    half = M // 2
    places = jnp.arange(half, dtype=jnp.float32) - (half - 1) / 2.0
    phase = jnp.pi * fraction * places[:, None] * sines[None, :]
    table = jnp.concatenate([jnp.cos(phase), jnp.sin(phase)], axis=0) * 1.4142135
    return table * gains[:, None]


def draw_steering(key, part):
    sines, fraction, gains = array_pieces(key)

    def one_table(items):
        return steer_columns(items[0], items[1], sines).astype(jnp.bfloat16)
    return lax.map(one_table, (fraction, gains))


def draw_data(key, part):
    sines, fraction, gains = array_pieces(key)
    chosen = jax.random.permutation(jax.random.fold_in(key, 104), G)[:SOURCES]
    picked = jnp.take(sines, chosen)
    bulk_edge = (1.0 + (M / K2) ** 0.5) ** 2
    ratio = jnp.exp(jax.random.uniform(jax.random.fold_in(key, 105), (F, SOURCES), jnp.float32, math.log(2.5), math.log(10.0)))
    levels = jnp.sqrt(bulk_edge * ratio / M)
    bin_keys = jax.random.split(jax.random.fold_in(key, 106), F)

    def one_bin(items):
        frac, gain, level, sub_key = items
        columns = steer_columns(frac, gain, picked)
        amp_key = jax.random.fold_in(sub_key, 1)
        noise_key = jax.random.fold_in(sub_key, 2)
        amps = jax.random.truncated_normal(amp_key, -4.0, 4.0, (K2, SOURCES), jnp.float32)
        noise = jax.random.truncated_normal(noise_key, -4.0, 4.0, (K2, M), jnp.float32)
        signal = jnp.dot(amps * level[None, :], columns.T, precision=lax.Precision.HIGHEST)
        return jnp.clip(signal + noise, -6.0, 6.0).astype(jnp.bfloat16)
    return lax.map(one_bin, (fraction, gains, levels, bin_keys))


def shard_levels(key, shape, cuts, least, high):
    def one(axis_at, blocks):
        steps = jax.random.uniform(jax.random.fold_in(jax.random.fold_in(key, 6), axis_at), (blocks,), jnp.float32, least / len(cuts), high / len(cuts))
        return jnp.repeat(jnp.exp(steps), shape[axis_at] // blocks).reshape((-1,) + (1,) * (len(shape) - axis_at - 1))

    factor_of = one(*cuts[0])
    for cut in cuts[1:]:
        factor_of = factor_of * one(*cut)
    return factor_of


def bell_draw(key, extent, width, reach, pieces=(), held_as=jnp.bfloat16):
    level = shard_levels(key, extent, pieces, -0.22, 0.18) if pieces else 1.0
    values = jax.random.normal(key, extent, jnp.float32) * width * level
    return jnp.minimum(jnp.maximum(values, -reach), reach).astype(held_as)


def setup_inputs(seed: int = 0) -> dict:
    seeds = jax.random.split(jax.random.key(seed), 4)
    data = draw_data(jax.random.fold_in(seeds[3], 71), 0)
    steering = draw_steering(jax.random.fold_in(seeds[3], 71), 0)
    start = bell_draw(seeds[2], (F, M, SOURCES), 1.0, 6.0, ((0, 256),), jnp.float32)
    return {"data": data, "steering": steering, "start": start}


def one_bin(snaps, steer, basis):
    covar = jnp.dot(snaps.T.astype(jnp.float32), snaps.astype(jnp.float32), preferred_element_type=jnp.float32) / snaps.shape[0]
    for step in range(ITERS):
        image = jnp.dot(covar, basis, precision=lax.Precision.HIGHEST)
        gram_mat = jnp.dot(image.T, image, precision=lax.Precision.HIGHEST)
        lower_factor = jnp.linalg.cholesky(gram_mat)
        basis = jax.scipy.linalg.solve_triangular(lower_factor, image.T, lower=True).T
    projector = jnp.dot(basis, basis.T, precision=lax.Precision.HIGHEST)
    basis_low = basis.astype(jnp.bfloat16)
    along = jnp.dot(basis_low.T.astype(jnp.float32), steer.astype(jnp.float32), preferred_element_type=jnp.float32)
    steer_wide = steer.astype(jnp.float32)
    energy = jnp.sum(steer_wide * steer_wide, axis=0)
    noise = energy - jnp.sum(along * along, axis=0)
    return (projector, noise)

def reference(data, steering, start):
    projector, noise = lax.map(lambda items: one_bin(items[0], items[1], items[2]), (data, steering, start))
    spectrum = F * M / jnp.sum(noise, axis=0)
    return (projector, spectrum)
```

```python
import functools

import jax
import jax.numpy as jnp
from jax import lax
from jax.experimental import pallas as pl
from jax.experimental.pallas import tpu as pltpu
from jax.sharding import Mesh
from jax.sharding import PartitionSpec as P

M = 1024
F = 256
G = 2048
N = 64
ITERS = 3
PARTS = 3
AXES = ("x", "yl", "z2", "z1", "z0", "yh", "c")
PLANE = ("x", "yl", "yh", "c")
PLANE_SIZE = 32
NT = (((1,), (1,)), ((), ()))
NN = (((1,), (0,)), ((), ()))


def dot(a, b, dims):
    return lax.dot_general(a, b, dims, preferred_element_type=jnp.float32)


def split(x, parts):
    out = []
    for _ in range(parts - 1):
        p = x.astype(jnp.bfloat16)
        out.append(p)
        x = x - p.astype(jnp.float32)
    return out + [x.astype(jnp.bfloat16)]


def fold(y, parts):
    s = y[0:N]
    for i in range(1, parts):
        s = s + y[i * N : (i + 1) * N]
    return s


def inverse_factor(gram, beside=None):
    row = lax.broadcasted_iota(jnp.int32, (8, 128), 0)
    lane = lax.broadcasted_iota(jnp.int32, (8, 128), 1)
    a = []
    for q in range(8):
        eye = jnp.where(lane - N == row + 8 * q, 1.0, 0.0).astype(jnp.float32)
        wide = jnp.concatenate([gram[8 * q : 8 * q + 8], jnp.zeros((8, N), jnp.float32)], axis=1)
        a.append(wide + eye)
    done = []
    for j in range(N):
        q0, s = divmod(j, 8)
        pivot_row = a[q0][s : s + 1, :]
        r = lax.rsqrt(jnp.broadcast_to(pivot_row[:, j : j + 1], (1, 128)))
        scaled = pivot_row * r
        done.append(scaled)
        for q in range(q0, 8):
            if q == q0 and s == 7:
                continue
            new = a[q] - (a[q][:, j : j + 1] * r) * scaled
            a[q] = jnp.where(row > s, new, a[q]) if q == q0 else new
        if beside is not None:
            beside(j)
    return jnp.concatenate(done, axis=0)[:, N:]


def subspace_kernel(d_ref, steer_ref, start_ref, noise_ref, left_ref, right_ref, energy_ref):
    def add_energy(j):
        rows = steer_ref[j * (M // N) : (j + 1) * (M // N), :].astype(jnp.float32)
        squares = rows * rows
        part = squares[0:8] + squares[8:16]
        energy_ref[...] = part if j == 0 else energy_ref[...] + part

    basis = start_ref[...]
    for step in range(ITERS):
        y = fold(dot(jnp.concatenate(split(basis, PARTS), 0), d_ref[...], NT), PARTS)
        x = fold(dot(jnp.concatenate(split(y, PARTS), 0), d_ref[...], NN), PARTS) * (1.0 / M)
        xs = jnp.concatenate(split(x, PARTS), 0)
        wide = fold(dot(xs, xs, NT), PARTS)
        gram = wide[:, 0:N]
        for i in range(1, PARTS):
            gram = gram + wide[:, N * i : N * (i + 1)]
        basis = lax.dot_general(
            inverse_factor(gram, add_energy if step == 0 else None),
            x,
            NN,
            precision=lax.Precision.HIGHEST,
            preferred_element_type=jnp.float32,
        )
    hi, lo = split(basis, 2)
    left_ref[...] = jnp.concatenate([hi, hi, lo, lo], 0)
    right_ref[...] = jnp.concatenate([hi, lo, hi, lo], 0)
    along = dot(hi, steer_ref[...], NN)
    energy = jnp.sum(energy_ref[...], axis=0, keepdims=True)
    noise = energy - jnp.sum(along * along, axis=0, keepdims=True)
    for c in range(G // 128):
        piece = noise[:, c * 128 : (c + 1) * 128]
        noise_ref[:, c, :] = jnp.broadcast_to(piece, (PLANE_SIZE, 128))


def subspace(d, steer, start):
    whole = pl.BlockSpec(memory_space=pltpu.VMEM)
    return pl.pallas_call(
        subspace_kernel,
        out_shape=(
            jax.ShapeDtypeStruct((PLANE_SIZE, G // 128, 128), jnp.float32),
            jax.ShapeDtypeStruct((4 * N, M), jnp.bfloat16),
            jax.ShapeDtypeStruct((4 * N, M), jnp.bfloat16),
        ),
        in_specs=[whole] * 3,
        out_specs=(whole, whole, whole),
        scratch_shapes=[pltpu.VMEM((8, G), jnp.float32)],
        compiler_params=pltpu.CompilerParams(vmem_limit_bytes=40 * 2**20),
        name="subspace",
    )(d, steer, start)


def on_device(data, steering, start):
    owned = lax.all_to_all(data, AXES, split_axis=0, concat_axis=0, tiled=True)
    owned = owned.reshape(M, M)
    noise, left, right = subspace(owned, steering[0], start[0].T)
    total = lax.all_to_all(noise, PLANE, split_axis=0, concat_axis=0, tiled=True).sum(0)
    for axis in ("z0", "z1", "z2"):
        total = total + lax.ppermute(total, axis, [(0, 1), (1, 0)])
    projector = lax.dot_general(
        left, right, (((0,), (0,)), ((), ())), preferred_element_type=jnp.float32
    )
    spectrum = F * M / total.reshape(G)
    return (projector[None], spectrum)


def solution(mesh):
    finer = Mesh(mesh.devices.reshape(4, 2, 2, 2, 2, 2, 2), AXES)
    by_bin = P(AXES, None, None)
    return jax.shard_map(
        on_device,
        mesh=finer,
        in_specs=(P(None, AXES, None), by_bin, by_bin),
        out_specs=(by_bin, P()),
        check_vma=False,
    )
```

```python
import functools

import jax
import jax.numpy as jnp
from jax import lax
from jax.experimental import pallas as pl
from jax.experimental.pallas import tpu as pltpu
from jax.sharding import Mesh
from jax.sharding import PartitionSpec as P

M = 1024
F = 256
G = 2048
N = 64
ITERS = 3
PARTS = 3
AXES = ("x", "yl", "z2", "z1", "z0", "yh", "c")
PLANE = ("x", "yl", "yh", "c")
PLANE_SIZE = 32
NT = (((1,), (1,)), ((), ()))
NN = (((1,), (0,)), ((), ()))


def dot(a, b, dims):
    return lax.dot_general(a, b, dims, preferred_element_type=jnp.float32)


def split(x, parts):
    out = []
    for _ in range(parts - 1):
        p = x.astype(jnp.bfloat16)
        out.append(p)
        x = x - p.astype(jnp.float32)
    return out + [x.astype(jnp.bfloat16)]


def fold(y, parts):
    s = y[0:N]
    for i in range(1, parts):
        s = s + y[i * N : (i + 1) * N]
    return s


def stacked(x):
    return jnp.concatenate(split(x, PARTS), 0)


def product(a, b):
    ah, am, al = split(a, 3)
    bh, bm, bl = split(b, 3)
    left = jnp.concatenate([ah, ah, am, am, ah, al], 1)
    right = jnp.concatenate([bh, bm, bh, bm, bl, bh], 0)
    return dot(left, right, NN)


def gram_of(xs):
    wide = fold(dot(xs, xs, NT), PARTS)
    gram = wide[:, 0:N]
    for i in range(1, PARTS):
        gram = gram + wide[:, N * i : N * (i + 1)]
    return gram


def lanes(x, j):
    return jnp.broadcast_to(x[:, j : j + 1], (8, 128))


def rows(x, s):
    return jnp.broadcast_to(x[s : s + 1, :], (8, 128))


def inverse_factor(gram, beside):
    row = lax.broadcasted_iota(jnp.int32, (8, 128), 0)
    lane = lax.broadcasted_iota(jnp.int32, (8, 128), 1)
    blocks = N // 8
    a = []
    for q in range(blocks):
        eye = jnp.where(lane - N == row + 8 * q, 1.0, 0.0).astype(jnp.float32)
        wide = jnp.concatenate([gram[8 * q : 8 * q + 8], jnp.zeros((8, N), jnp.float32)], axis=1)
        a.append(wide + eye)
    done = []
    for k in range(blocks):
        below = range(k, blocks)
        cols = [[lanes(a[q], 8 * k + i) for q in below] for i in range(8)]
        scaled = []
        for i in range(8):
            r = lax.rsqrt(rows(cols[i][0], i))
            l = [c * r for c in cols[i]]
            cols[i] = l
            for i2 in range(i + 1, 8):
                t = rows(l[0], i2)
                cols[i2] = [c - m * t for c, m in zip(cols[i2], l)]
            this = rows(a[k], i)
            for i1 in range(i):
                this = this - rows(cols[i1][0], i) * scaled[i1]
            scaled.append(this * r)
        out = scaled[0]
        for i in range(1, 8):
            out = jnp.where(row == i, scaled[i], out)
        done.append(out)
        for q in range(k + 1, blocks):
            for i in range(8):
                a[q] = a[q] - cols[i][q - k] * scaled[i]
        beside(k)
    return jnp.concatenate(done, axis=0)[:, N:]


def subspace_kernel(d_ref, steer_hbm, start_ref, noise_ref, left_ref, right_ref, steer_ref, y_ref, w_ref, energy_ref, sem):
    fetch = pltpu.make_async_copy(steer_hbm, steer_ref, sem)
    fetch.start()

    def back(s, j):
        cut = pl.ds(j * (M // 4), M // 4)
        y_ref[:, cut] = fold(dot(s, d_ref[cut, :], NT), PARTS)

    def forth(s, j):
        cut = pl.ds(j * (M // 4), M // 4)
        w_ref[:, cut] = fold(dot(s, d_ref[:, cut], NN), PARTS) * (1.0 / M)

    def add_energy(j):
        block = steer_ref[j * (M // 8) : (j + 1) * (M // 8), :].astype(jnp.float32)
        squares = block * block
        part = jnp.sum(squares.reshape(M // 64, 8, G), axis=0)
        energy_ref[...] = part if j == 0 else energy_ref[...] + part

    ss = stacked(start_ref[...])
    for j in range(4):
        back(ss, j)
    ss = stacked(y_ref[...])
    for j in range(4):
        forth(ss, j)
    x = w_ref[...]
    for step in range(ITERS):
        xs = stacked(x)
        last = step == ITERS - 1
        held = [None]

        def beside(k):
            if last:
                add_energy(k)
            elif k < 4:
                back(xs, k)
            else:
                if k == 4:
                    held[0] = stacked(y_ref[...])
                forth(held[0], k - 4)

        if last:
            fetch.wait()
        inverse = inverse_factor(gram_of(xs), beside)
        x = product(inverse, x if last else w_ref[...])
    hi, lo = split(x, 2)
    left_ref[...] = jnp.concatenate([hi, hi, lo, lo], 0)
    right_ref[...] = jnp.concatenate([hi, lo, hi, lo], 0)
    along = dot(hi, steer_ref[...], NN)
    energy = jnp.sum(energy_ref[...], axis=0, keepdims=True)
    noise = energy - jnp.sum(along * along, axis=0, keepdims=True)
    for c in range(G // 128):
        piece = noise[:, c * 128 : (c + 1) * 128]
        noise_ref[:, c, :] = jnp.broadcast_to(piece, (PLANE_SIZE, 128))


def subspace(d, steer, start):
    whole = pl.BlockSpec(memory_space=pltpu.VMEM)
    return pl.pallas_call(
        subspace_kernel,
        out_shape=(
            jax.ShapeDtypeStruct((PLANE_SIZE, G // 128, 128), jnp.float32),
            jax.ShapeDtypeStruct((4 * N, M), jnp.bfloat16),
            jax.ShapeDtypeStruct((4 * N, M), jnp.bfloat16),
        ),
        in_specs=[whole, pl.BlockSpec(memory_space=pltpu.HBM), whole],
        out_specs=(whole, whole, whole),
        scratch_shapes=[
            pltpu.VMEM((M, G), jnp.bfloat16),
            pltpu.VMEM((N, M), jnp.float32),
            pltpu.VMEM((N, M), jnp.float32),
            pltpu.VMEM((8, G), jnp.float32),
            pltpu.SemaphoreType.DMA,
        ],
        compiler_params=pltpu.CompilerParams(vmem_limit_bytes=40 * 2**20),
        name="subspace",
    )(d, steer, start)


def on_device(data, steering, start):
    owned = lax.all_to_all(data, AXES, split_axis=0, concat_axis=0, tiled=True)
    owned = owned.reshape(M, M)
    noise, left, right = subspace(owned, steering[0], start[0].T)
    total = lax.all_to_all(noise, PLANE, split_axis=0, concat_axis=0, tiled=True).sum(0)
    for axis in ("z0", "z1", "z2"):
        total = total + lax.ppermute(total, axis, [(0, 1), (1, 0)])
    projector = lax.dot_general(
        left, right, (((0,), (0,)), ((), ())), preferred_element_type=jnp.float32
    )
    spectrum = F * M / total.reshape(G)
    return (projector[None], spectrum)


def solution(mesh):
    finer = Mesh(mesh.devices.reshape(4, 2, 2, 2, 2, 2, 2), AXES)
    by_bin = P(AXES, None, None)
    return jax.shard_map(
        on_device,
        mesh=finer,
        in_specs=(P(None, AXES, None), by_bin, by_bin),
        out_specs=(by_bin, P()),
        check_vma=False,
    )
```

```python
import functools

import jax
import jax.numpy as jnp
from jax import lax
from jax.experimental import pallas as pl
from jax.experimental.pallas import tpu as pltpu
from jax.sharding import Mesh
from jax.sharding import PartitionSpec as P

M = 1024
F = 256
G = 2048
N = 64
ITERS = 3
PARTS = 3
CHUNKS = 4
AXES = ("x", "yl", "z2", "z1", "z0", "yh", "c")
PLANE = ("x", "yl", "yh", "c")
PLANE_SIZE = 32
NT = (((1,), (1,)), ((), ()))
NN = (((1,), (0,)), ((), ()))


def dot(a, b, dims):
    return lax.dot_general(a, b, dims, preferred_element_type=jnp.float32)


def split(x, parts):
    out = []
    for _ in range(parts - 1):
        p = x.astype(jnp.bfloat16)
        out.append(p)
        x = x - p.astype(jnp.float32)
    return out + [x.astype(jnp.bfloat16)]


def fold(y, parts):
    s = y[0:N]
    for i in range(1, parts):
        s = s + y[i * N : (i + 1) * N]
    return s


def stacked(x):
    return jnp.concatenate(split(x, PARTS), 0)


def product(a, b):
    ah, am, al = split(a, 3)
    bh, bm, bl = split(b, 3)
    left = jnp.concatenate([ah, ah, am, am, ah, al], 1)
    right = jnp.concatenate([bh, bm, bh, bm, bl, bh], 0)
    return dot(left, right, NN)


def gram_of(xs):
    wide = fold(dot(xs, xs, NT), PARTS)
    gram = wide[:, 0:N]
    for i in range(1, PARTS):
        gram = gram + wide[:, N * i : N * (i + 1)]
    return gram


def lanes(x, j):
    return jnp.broadcast_to(x[:, j : j + 1], (8, 128))


def rows(x, s):
    return jnp.broadcast_to(x[s : s + 1, :], (8, 128))


def inverse_factor(gram, beside):
    row = lax.broadcasted_iota(jnp.int32, (8, 128), 0)
    lane = lax.broadcasted_iota(jnp.int32, (8, 128), 1)
    blocks = N // 8
    a = []
    for q in range(blocks):
        eye = jnp.where(lane - N == row + 8 * q, 1.0, 0.0).astype(jnp.float32)
        wide = jnp.concatenate([gram[8 * q : 8 * q + 8], jnp.zeros((8, N), jnp.float32)], axis=1)
        a.append(wide + eye)
    done = []
    for k in range(blocks):
        below = range(k, blocks)
        cols = [[lanes(a[q], 8 * k + i) for q in below] for i in range(8)]
        scaled = []
        for i in range(8):
            r = lax.rsqrt(rows(cols[i][0], i))
            l = [c * r for c in cols[i]]
            cols[i] = l
            for i2 in range(i + 1, 8):
                t = rows(l[0], i2)
                cols[i2] = [c - m * t for c, m in zip(cols[i2], l)]
            this = rows(a[k], i)
            for i1 in range(i):
                this = this - rows(cols[i1][0], i) * scaled[i1]
            scaled.append(this * r)
        out = scaled[0]
        for i in range(1, 8):
            out = jnp.where(row == i, scaled[i], out)
        done.append(out)
        for q in range(k + 1, blocks):
            for i in range(8):
                a[q] = a[q] - cols[i][q - k] * scaled[i]
        beside(k)
    return jnp.concatenate(done, axis=0)[:, N:]


def subspace_kernel(
    data_ref, steer_hbm, start_ref, noise_ref, left_ref, right_ref, d_ref, steer_ref, y_ref, w_ref, energy_ref, sem
):
    per = F // CHUNKS
    fetch = pltpu.make_async_copy(steer_hbm, steer_ref, sem)
    fetch.start()

    def back(s, j):
        cut = pl.ds(j * (M // 4), M // 4)
        y_ref[:, cut] = fold(dot(s, d_ref[cut, :], NT), PARTS)

    def forth(s, j):
        cut = pl.ds(j * (M // 4), M // 4)
        w_ref[:, cut] = fold(dot(s, d_ref[:, cut], NN), PARTS) * (1.0 / M)

    def add_energy(j):
        block = steer_ref[j * (M // 8) : (j + 1) * (M // 8), :].astype(jnp.float32)
        squares = block * block
        part = jnp.sum(squares.reshape(M // 64, 8, G), axis=0)
        energy_ref[...] = part if j == 0 else energy_ref[...] + part

    ss = stacked(start_ref[...])
    for j in range(CHUNKS):
        d_ref[j * per * 4 : (j + 1) * per * 4, :] = data_ref[j * per : (j + 1) * per].reshape(per * 4, M)
        back(ss, j)
    ss = stacked(y_ref[...])
    for j in range(4):
        forth(ss, j)
    x = w_ref[...]
    for step in range(ITERS):
        xs = stacked(x)
        last = step == ITERS - 1
        held = [None]

        def beside(k):
            if last:
                add_energy(k)
            elif k < 4:
                back(xs, k)
            else:
                if k == 4:
                    held[0] = stacked(y_ref[...])
                forth(held[0], k - 4)

        if last:
            fetch.wait()
        inverse = inverse_factor(gram_of(xs), beside)
        x = product(inverse, x if last else w_ref[...])
    hi, lo = split(x, 2)
    left_ref[...] = jnp.concatenate([hi, hi, lo, lo], 0)
    right_ref[...] = jnp.concatenate([hi, lo, hi, lo], 0)
    along = dot(hi, steer_ref[...], NN)
    energy = jnp.sum(energy_ref[...], axis=0, keepdims=True)
    noise = energy - jnp.sum(along * along, axis=0, keepdims=True)
    for c in range(G // 128):
        piece = noise[:, c * 128 : (c + 1) * 128]
        noise_ref[:, c, :] = jnp.broadcast_to(piece, (PLANE_SIZE, 128))


def subspace(data, steer, start):
    whole = pl.BlockSpec(memory_space=pltpu.VMEM)
    far = pl.BlockSpec(memory_space=pltpu.HBM)
    return pl.pallas_call(
        subspace_kernel,
        out_shape=(
            jax.ShapeDtypeStruct((PLANE_SIZE, G // 128, 128), jnp.float32),
            jax.ShapeDtypeStruct((4 * N, M), jnp.bfloat16),
            jax.ShapeDtypeStruct((4 * N, M), jnp.bfloat16),
        ),
        in_specs=[whole, far, whole],
        out_specs=(whole, whole, whole),
        scratch_shapes=[
            pltpu.VMEM((M, M), jnp.bfloat16),
            pltpu.VMEM((M, G), jnp.bfloat16),
            pltpu.VMEM((N, M), jnp.float32),
            pltpu.VMEM((N, M), jnp.float32),
            pltpu.VMEM((8, G), jnp.float32),
            pltpu.SemaphoreType.DMA,
        ],
        compiler_params=pltpu.CompilerParams(vmem_limit_bytes=52_000_000),
        name="subspace",
    )(data, steer, start)


def on_device(data, steering, start):
    owned = lax.all_to_all(data, AXES, split_axis=0, concat_axis=0, tiled=True)
    noise, left, right = subspace(owned, steering[0], start[0].T)
    total = lax.all_to_all(noise, PLANE, split_axis=0, concat_axis=0, tiled=True).sum(0)
    for axis in ("z0", "z1"):
        total = total + lax.ppermute(total, axis, [(0, 1), (1, 0)])
    total = total + lax.ppermute(total, ("z2", "z1", "z0"), [(z, 7 - z) for z in range(8)])
    projector = lax.dot_general(
        left, right, (((0,), (0,)), ((), ())), preferred_element_type=jnp.float32
    )
    spectrum = F * M / total.reshape(G)
    return (projector[None], spectrum)


def solution(mesh):
    finer = Mesh(mesh.devices.reshape(4, 2, 2, 2, 2, 2, 2), AXES)
    by_bin = P(AXES, None, None)
    return jax.shard_map(
        on_device,
        mesh=finer,
        in_specs=(P(None, AXES, None), by_bin, by_bin),
        out_specs=(by_bin, P()),
        check_vma=False,
    )
```

```python
import functools

import jax
import jax.numpy as jnp
from jax import lax
from jax.experimental import pallas as pl
from jax.experimental.pallas import tpu as pltpu
from jax.sharding import Mesh
from jax.sharding import PartitionSpec as P

M = 1024
F = 256
G = 2048
N = 64
ITERS = 3
PARTS = 3
CHUNKS = 4
WIDTHS = (8, 8, 16, 16, 16)
AXES = ("x", "yl", "z2", "z1", "z0", "yh", "c")
PLANE = ("x", "yl", "yh", "c")
PLANE_SIZE = 32
NT = (((1,), (1,)), ((), ()))
NN = (((1,), (0,)), ((), ()))


def dot(a, b, dims):
    return lax.dot_general(a, b, dims, preferred_element_type=jnp.float32)


def split(x, parts):
    out = []
    for _ in range(parts - 1):
        p = x.astype(jnp.bfloat16)
        out.append(p)
        x = x - p.astype(jnp.float32)
    return out + [x.astype(jnp.bfloat16)]


def fold(y, parts):
    s = y[0:N]
    for i in range(1, parts):
        s = s + y[i * N : (i + 1) * N]
    return s


def stacked(x):
    return jnp.concatenate(split(x, PARTS), 0)


def product(a, b):
    ah, am, al = split(a, 3)
    bh, bm, bl = split(b, 3)
    left = jnp.concatenate([ah, ah, am, am, ah, al], 1)
    right = jnp.concatenate([bh, bm, bh, bm, bl, bh], 0)
    return dot(left, right, NN)


def gram_of(xs):
    wide = fold(dot(xs, xs, NT), PARTS)
    gram = wide[:, 0:N]
    for i in range(1, PARTS):
        gram = gram + wide[:, N * i : N * (i + 1)]
    return gram


def lanes(x, j):
    return jnp.broadcast_to(x[:, j : j + 1], (8, 128))


def rows(x, s):
    return jnp.broadcast_to(x[s : s + 1, :], (8, 128))


def inverse_factor(gram, beside):
    row = lax.broadcasted_iota(jnp.int32, (8, 128), 0)
    lane = lax.broadcasted_iota(jnp.int32, (8, 128), 1)
    blocks = N // 8
    a = []
    for q in range(blocks):
        eye = jnp.where(lane - N == row + 8 * q, 1.0, 0.0).astype(jnp.float32)
        wide = jnp.concatenate([gram[8 * q : 8 * q + 8], jnp.zeros((8, N), jnp.float32)], axis=1)
        a.append(wide + eye)
    done = []
    first = 0
    for width in WIDTHS:
        top = first // 8
        near = width // 8
        cols = [[lanes(a[q], first + i) if q >= top + i // 8 else None for q in range(top, blocks)] for i in range(width)]
        scaled = []
        for i in range(width):
            g = i // 8
            r = lax.rsqrt(rows(cols[i][g], i % 8))
            cols[i] = [None if c is None else c * r for c in cols[i]]
            l = cols[i]
            for i2 in range(i + 1, width):
                t = rows(l[i2 // 8], i2 % 8)
                cols[i2] = [None if c is None else c - m * t for c, m in zip(cols[i2], l)]
            this = rows(a[top + g], i % 8)
            for i1 in range(i):
                this = this - rows(cols[i1][g], i % 8) * scaled[i1]
            scaled.append(this * r)
        for g in range(near):
            out = scaled[8 * g]
            for i in range(1, 8):
                out = jnp.where(row == i, scaled[8 * g + i], out)
            done.append(out)
        for q in range(top + near, blocks):
            for i in range(width):
                a[q] = a[q] - cols[i][q - top] * scaled[i]
        for g in range(near):
            beside(top + g)
        first += width
    return jnp.concatenate(done, axis=0)[:, N:]


def subspace_kernel(
    data_ref, steer_hbm, start_ref, noise_ref, left_ref, right_ref, d_ref, steer_ref, y_ref, w_ref, energy_ref, sem
):
    per = F // CHUNKS
    fetch = pltpu.make_async_copy(steer_hbm, steer_ref, sem)
    fetch.start()

    def back(s, j):
        cut = pl.ds(j * (M // 4), M // 4)
        y_ref[:, cut] = fold(dot(s, d_ref[cut, :], NT), PARTS)

    def forth(s, j):
        cut = pl.ds(j * (M // 4), M // 4)
        w_ref[:, cut] = fold(dot(s, d_ref[:, cut], NN), PARTS) * (1.0 / M)

    def add_energy(j):
        block = steer_ref[j * (M // 8) : (j + 1) * (M // 8), :].astype(jnp.float32)
        squares = block * block
        part = jnp.sum(squares.reshape(M // 64, 8, G), axis=0)
        energy_ref[...] = part if j == 0 else energy_ref[...] + part

    ss = stacked(start_ref[...])
    for j in range(CHUNKS):
        d_ref[j * per * 4 : (j + 1) * per * 4, :] = data_ref[j * per : (j + 1) * per].reshape(per * 4, M)
        back(ss, j)
    ss = stacked(y_ref[...])
    for j in range(4):
        forth(ss, j)
    x = w_ref[...]
    for step in range(ITERS):
        xs = stacked(x)
        last = step == ITERS - 1
        held = [None]

        def beside(k):
            if last:
                add_energy(k)
            elif k < 4:
                back(xs, k)
            else:
                if k == 4:
                    held[0] = stacked(y_ref[...])
                forth(held[0], k - 4)

        if last:
            fetch.wait()
        inverse = inverse_factor(gram_of(xs), beside)
        x = product(inverse, x if last else w_ref[...])
    hi, lo = split(x, 2)
    left_ref[...] = jnp.concatenate([hi, hi, lo, lo], 0)
    right_ref[...] = jnp.concatenate([hi, lo, hi, lo], 0)
    along = dot(hi, steer_ref[...], NN)
    energy = jnp.sum(energy_ref[...], axis=0, keepdims=True)
    noise = energy - jnp.sum(along * along, axis=0, keepdims=True)
    for c in range(G // 128):
        piece = noise[:, c * 128 : (c + 1) * 128]
        noise_ref[:, c, :] = jnp.broadcast_to(piece, (PLANE_SIZE, 128))


def subspace(data, steer, start):
    whole = pl.BlockSpec(memory_space=pltpu.VMEM)
    far = pl.BlockSpec(memory_space=pltpu.HBM)
    return pl.pallas_call(
        subspace_kernel,
        out_shape=(
            jax.ShapeDtypeStruct((PLANE_SIZE, G // 128, 128), jnp.float32),
            jax.ShapeDtypeStruct((4 * N, M), jnp.bfloat16),
            jax.ShapeDtypeStruct((4 * N, M), jnp.bfloat16),
        ),
        in_specs=[whole, far, whole],
        out_specs=(whole, whole, whole),
        scratch_shapes=[
            pltpu.VMEM((M, M), jnp.bfloat16),
            pltpu.VMEM((M, G), jnp.bfloat16),
            pltpu.VMEM((N, M), jnp.float32),
            pltpu.VMEM((N, M), jnp.float32),
            pltpu.VMEM((8, G), jnp.float32),
            pltpu.SemaphoreType.DMA,
        ],
        compiler_params=pltpu.CompilerParams(vmem_limit_bytes=52_000_000),
        name="subspace",
    )(data, steer, start)


def on_device(data, steering, start):
    owned = lax.all_to_all(data, AXES, split_axis=0, concat_axis=0, tiled=True)
    noise, left, right = subspace(owned, steering[0], start[0].T)
    total = lax.all_to_all(noise, PLANE, split_axis=0, concat_axis=0, tiled=True).sum(0)
    swap = [(0, 1), (1, 0)]
    one = lax.ppermute(total, "z0", swap)
    two = lax.ppermute(total, "z1", swap)
    three = lax.ppermute(total, ("z1", "z0"), [(z, 3 - z) for z in range(4)])
    total = (total + one) + (two + three)
    total = total + lax.ppermute(total, ("z2", "z1", "z0"), [(z, 7 - z) for z in range(8)])
    projector = lax.dot_general(
        left, right, (((0,), (0,)), ((), ())), preferred_element_type=jnp.float32
    )
    spectrum = F * M / total.reshape(G)
    return (projector[None], spectrum)


def solution(mesh):
    finer = Mesh(mesh.devices.reshape(4, 2, 2, 2, 2, 2, 2), AXES)
    by_bin = P(AXES, None, None)
    return jax.shard_map(
        on_device,
        mesh=finer,
        in_specs=(P(None, AXES, None), by_bin, by_bin),
        out_specs=(by_bin, P()),
        check_vma=False,
    )
```

```python
import functools

import jax
import jax.numpy as jnp
from jax import lax
from jax.experimental import pallas as pl
from jax.experimental.pallas import tpu as pltpu
from jax.sharding import Mesh
from jax.sharding import PartitionSpec as P

M = 1024
F = 256
G = 2048
N = 64
ITERS = 3
PARTS = 3
CHUNKS = 4
WIDTHS = (8, 8, 16, 16, 16)
AXES = ("x", "yl", "z2", "z1", "z0", "yh", "c")
PLANE = ("x", "yl", "yh", "c")
PLANE_SIZE = 32
NT = (((1,), (1,)), ((), ()))
NN = (((1,), (0,)), ((), ()))


def dot(a, b, dims):
    return lax.dot_general(a, b, dims, preferred_element_type=jnp.float32)


def split(x, parts):
    out = []
    for _ in range(parts - 1):
        p = x.astype(jnp.bfloat16)
        out.append(p)
        x = x - p.astype(jnp.float32)
    return out + [x.astype(jnp.bfloat16)]


def fold(y, parts):
    s = y[0:N]
    for i in range(1, parts):
        s = s + y[i * N : (i + 1) * N]
    return s


def stacked(x):
    return jnp.concatenate(split(x, PARTS), 0)


def product(a, b):
    ah, am, al = split(a, 3)
    bh, bm, bl = split(b, 3)
    left = jnp.concatenate([ah, ah, am, am, ah, al], 1)
    right = jnp.concatenate([bh, bm, bh, bm, bl, bh], 0)
    return dot(left, right, NN)


def gram_of(xs):
    wide = fold(dot(xs, xs, NT), PARTS)
    gram = wide[:, 0:N]
    for i in range(1, PARTS):
        gram = gram + wide[:, N * i : N * (i + 1)]
    return gram


def lanes(x, j):
    return jnp.broadcast_to(x[:, j : j + 1], (8, 128))


def rows(x, s):
    return jnp.broadcast_to(x[s : s + 1, :], (8, 128))


def inverse_factor(gram, beside):
    row = lax.broadcasted_iota(jnp.int32, (8, 128), 0)
    lane = lax.broadcasted_iota(jnp.int32, (8, 128), 1)
    blocks = N // 8
    a = []
    for q in range(blocks):
        eye = jnp.where(lane - N == row + 8 * q, 1.0, 0.0).astype(jnp.float32)
        wide = jnp.concatenate([gram[8 * q : 8 * q + 8], jnp.zeros((8, N), jnp.float32)], axis=1)
        a.append(wide + eye)
    done = []
    first = 0
    for width in WIDTHS:
        top = first // 8
        near = width // 8
        cols = [[lanes(a[q], first + i) if q >= top + i // 8 else None for q in range(top, blocks)] for i in range(width)]
        scaled = []
        factor = [[] for _ in range(width)]
        for i in range(0, width, 2):
            g = i // 8
            one = rows(cols[i][g], i % 8)
            cross = rows(cols[i][g], i % 8 + 1)
            two = rows(cols[i + 1][g], i % 8 + 1)
            r1 = lax.rsqrt(one)
            t = cross * r1
            r2 = lax.rsqrt(two - t * t)
            cols[i] = [None if c is None else c * r1 for c in cols[i]]
            cols[i + 1] = [None if c is None else (c - m * t) * r2 for c, m in zip(cols[i + 1], cols[i])]
            factor[i + 1].append(t)
            for i2 in range(i + 2, width):
                t1 = rows(cols[i][i2 // 8], i2 % 8)
                t2 = rows(cols[i + 1][i2 // 8], i2 % 8)
                factor[i2] += [t1, t2]
                cols[i2] = [None if c is None else c - (m1 * t1 + m2 * t2) for c, m1, m2 in zip(cols[i2], cols[i], cols[i + 1])]
            for s, r in ((i, r1), (i + 1, r2)):
                this = rows(a[top + g], s % 8)
                for t, line in zip(factor[s], scaled):
                    this = this - t * line
                scaled.append(this * r)
        for g in range(near):
            out = scaled[8 * g]
            for i in range(1, 8):
                out = jnp.where(row == i, scaled[8 * g + i], out)
            done.append(out)
        for q in range(top + near, blocks):
            for i in range(width):
                a[q] = a[q] - cols[i][q - top] * scaled[i]
        for g in range(near):
            beside(top + g)
        first += width
    return jnp.concatenate(done, axis=0)[:, N:]


def subspace_kernel(
    data_ref, steer_hbm, start_ref, noise_ref, left_ref, right_ref, d_ref, steer_ref, y_ref, w_ref, energy_ref, sem
):
    per = F // CHUNKS
    fetch = pltpu.make_async_copy(steer_hbm, steer_ref, sem)
    fetch.start()

    def back(s, j):
        cut = pl.ds(j * (M // 4), M // 4)
        y_ref[:, cut] = fold(dot(s, d_ref[cut, :], NT), PARTS)

    def forth(s, j):
        cut = pl.ds(j * (M // 4), M // 4)
        w_ref[:, cut] = fold(dot(s, d_ref[:, cut], NN), PARTS) * (1.0 / M)

    def add_energy(j):
        block = steer_ref[j * (M // 8) : (j + 1) * (M // 8), :].astype(jnp.float32)
        squares = block * block
        part = jnp.sum(squares.reshape(M // 64, 8, G), axis=0)
        energy_ref[...] = part if j == 0 else energy_ref[...] + part

    ss = stacked(start_ref[...])
    for j in range(CHUNKS):
        d_ref[j * per * 4 : (j + 1) * per * 4, :] = data_ref[j * per : (j + 1) * per].reshape(per * 4, M)
        back(ss, j)
    ss = stacked(y_ref[...])
    for j in range(4):
        forth(ss, j)
    x = w_ref[...]
    for step in range(ITERS):
        xs = stacked(x)
        last = step == ITERS - 1
        held = [None]

        def beside(k):
            if last:
                add_energy(k)
            elif k < 4:
                back(xs, k)
            else:
                if k == 4:
                    held[0] = stacked(y_ref[...])
                forth(held[0], k - 4)

        if last:
            fetch.wait()
        inverse = inverse_factor(gram_of(xs), beside)
        x = product(inverse, x if last else w_ref[...])
    hi, lo = split(x, 2)
    left_ref[...] = jnp.concatenate([hi, hi, lo, lo], 0)
    right_ref[...] = jnp.concatenate([hi, lo, hi, lo], 0)
    along = dot(hi, steer_ref[...], NN)
    energy = jnp.sum(energy_ref[...], axis=0, keepdims=True)
    noise = energy - jnp.sum(along * along, axis=0, keepdims=True)
    for c in range(G // 128):
        piece = noise[:, c * 128 : (c + 1) * 128]
        noise_ref[:, c, :] = jnp.broadcast_to(piece, (PLANE_SIZE, 128))


def subspace(data, steer, start):
    whole = pl.BlockSpec(memory_space=pltpu.VMEM)
    far = pl.BlockSpec(memory_space=pltpu.HBM)
    return pl.pallas_call(
        subspace_kernel,
        out_shape=(
            jax.ShapeDtypeStruct((PLANE_SIZE, G // 128, 128), jnp.float32),
            jax.ShapeDtypeStruct((4 * N, M), jnp.bfloat16),
            jax.ShapeDtypeStruct((4 * N, M), jnp.bfloat16),
        ),
        in_specs=[whole, far, whole],
        out_specs=(whole, whole, whole),
        scratch_shapes=[
            pltpu.VMEM((M, M), jnp.bfloat16),
            pltpu.VMEM((M, G), jnp.bfloat16),
            pltpu.VMEM((N, M), jnp.float32),
            pltpu.VMEM((N, M), jnp.float32),
            pltpu.VMEM((8, G), jnp.float32),
            pltpu.SemaphoreType.DMA,
        ],
        compiler_params=pltpu.CompilerParams(vmem_limit_bytes=52_000_000),
        name="subspace",
    )(data, steer, start)


def on_device(data, steering, start):
    owned = lax.all_to_all(data, AXES, split_axis=0, concat_axis=0, tiled=True)
    noise, left, right = subspace(owned, steering[0], start[0].T)
    total = lax.all_to_all(noise, PLANE, split_axis=0, concat_axis=0, tiled=True).sum(0)
    swap = [(0, 1), (1, 0)]
    one = lax.ppermute(total, "z0", swap)
    two = lax.ppermute(total, "z1", swap)
    three = lax.ppermute(total, ("z1", "z0"), [(z, 3 - z) for z in range(4)])
    total = (total + one) + (two + three)
    total = total + lax.ppermute(total, ("z2", "z1", "z0"), [(z, 7 - z) for z in range(8)])
    projector = lax.dot_general(
        left, right, (((0,), (0,)), ((), ())), preferred_element_type=jnp.float32
    )
    spectrum = F * M / total.reshape(G)
    return (projector[None], spectrum)


def solution(mesh):
    finer = Mesh(mesh.devices.reshape(4, 2, 2, 2, 2, 2, 2), AXES)
    by_bin = P(AXES, None, None)
    return jax.shard_map(
        on_device,
        mesh=finer,
        in_specs=(P(None, AXES, None), by_bin, by_bin),
        out_specs=(by_bin, P()),
        check_vma=False,
    )
```

```python
import functools

import jax
import jax.numpy as jnp
from jax import lax
from jax.experimental import pallas as pl
from jax.experimental.pallas import tpu as pltpu
from jax.sharding import Mesh
from jax.sharding import PartitionSpec as P

M = 1024
F = 256
G = 2048
N = 64
ITERS = 3
PARTS = 3
CHUNKS = 4
WIDTHS = (16, 16, 16, 16)
AXES = ("x", "yl", "z2", "z1", "z0", "yh", "c")
PLANE = ("x", "yl", "yh", "c")
PLANE_SIZE = 32
NT = (((1,), (1,)), ((), ()))
NN = (((1,), (0,)), ((), ()))


def dot(a, b, dims):
    return lax.dot_general(a, b, dims, preferred_element_type=jnp.float32)


def split(x, parts):
    out = []
    for _ in range(parts - 1):
        p = x.astype(jnp.bfloat16)
        out.append(p)
        x = x - p.astype(jnp.float32)
    return out + [x.astype(jnp.bfloat16)]


def fold(y, parts):
    s = y[0:N]
    for i in range(1, parts):
        s = s + y[i * N : (i + 1) * N]
    return s


def stacked(x):
    return jnp.concatenate(split(x, PARTS), 0)


def product(a, b):
    ah, am, al = split(a, 3)
    bh, bm, bl = split(b, 3)
    left = jnp.concatenate([ah, ah, am, am, ah, al], 1)
    right = jnp.concatenate([bh, bm, bh, bm, bl, bh], 0)
    return dot(left, right, NN)


def gram_of(xs):
    wide = fold(dot(xs, xs, NT), PARTS)
    gram = wide[:, 0:N]
    for i in range(1, PARTS):
        gram = gram + wide[:, N * i : N * (i + 1)]
    return gram


def lanes(x, j):
    return jnp.broadcast_to(x[:, j : j + 1], (8, 128))


def rows(x, s):
    return jnp.broadcast_to(x[s : s + 1, :], (8, 128))


def inverse_factor(gram, beside):
    row = lax.broadcasted_iota(jnp.int32, (8, 128), 0)
    lane = lax.broadcasted_iota(jnp.int32, (8, 128), 1)
    blocks = N // 8
    a = []
    for q in range(blocks):
        eye = jnp.where(lane - N == row + 8 * q, 1.0, 0.0).astype(jnp.float32)
        wide = jnp.concatenate([gram[8 * q : 8 * q + 8], jnp.zeros((8, N), jnp.float32)], axis=1)
        a.append(wide + eye)
    done = []
    first = 0
    for width in WIDTHS:
        top = first // 8
        near = width // 8
        cols = [[lanes(a[q], first + i) if q >= top + i // 8 else None for q in range(top, blocks)] for i in range(width)]
        scaled = []
        factor = [[] for _ in range(width)]
        for i in range(0, width, 2):
            g = i // 8
            one = rows(cols[i][g], i % 8)
            cross = rows(cols[i][g], i % 8 + 1)
            two = rows(cols[i + 1][g], i % 8 + 1)
            r1 = lax.rsqrt(one)
            t = cross * r1
            r2 = lax.rsqrt(two - t * t)
            cols[i] = [None if c is None else c * r1 for c in cols[i]]
            cols[i + 1] = [None if c is None else (c - m * t) * r2 for c, m in zip(cols[i + 1], cols[i])]
            factor[i + 1].append(t)
            for i2 in range(i + 2, width):
                t1 = rows(cols[i][i2 // 8], i2 % 8)
                t2 = rows(cols[i + 1][i2 // 8], i2 % 8)
                factor[i2] += [t1, t2]
                cols[i2] = [None if c is None else c - (m1 * t1 + m2 * t2) for c, m1, m2 in zip(cols[i2], cols[i], cols[i + 1])]
            for s, r in ((i, r1), (i + 1, r2)):
                this = rows(a[top + g], s % 8)
                for t, line in zip(factor[s], scaled):
                    this = this - t * line
                scaled.append(this * r)
        for g in range(near):
            out = scaled[8 * g]
            for i in range(1, 8):
                out = jnp.where(row == i, scaled[8 * g + i], out)
            done.append(out)
        for q in range(top + near, blocks):
            for i in range(width):
                a[q] = a[q] - cols[i][q - top] * scaled[i]
        for g in range(near):
            beside(top + g)
        first += width
    return jnp.concatenate(done, axis=0)[:, N:]


def subspace_kernel(
    data_ref, steer_hbm, start_ref, noise_ref, left_ref, right_ref, d_ref, steer_ref, y_ref, w_ref, energy_ref, sem
):
    per = F // CHUNKS
    fetch = pltpu.make_async_copy(steer_hbm, steer_ref, sem)
    fetch.start()

    def back(s, j):
        cut = pl.ds(j * (M // 4), M // 4)
        y_ref[:, cut] = fold(dot(s, d_ref[cut, :], NT), PARTS)

    def forth(s, j):
        cut = pl.ds(j * (M // 4), M // 4)
        w_ref[:, cut] = fold(dot(s, d_ref[:, cut], NN), PARTS) * (1.0 / M)

    def add_energy(j):
        block = steer_ref[j * (M // 8) : (j + 1) * (M // 8), :].astype(jnp.float32)
        squares = block * block
        part = jnp.sum(squares.reshape(M // 64, 8, G), axis=0)
        energy_ref[...] = part if j == 0 else energy_ref[...] + part

    ss = stacked(start_ref[...])
    for j in range(CHUNKS):
        d_ref[j * per * 4 : (j + 1) * per * 4, :] = data_ref[j * per : (j + 1) * per].reshape(per * 4, M)
        back(ss, j)
    ss = stacked(y_ref[...])
    for j in range(4):
        forth(ss, j)
    x = w_ref[...]
    for step in range(ITERS):
        xs = stacked(x)
        last = step == ITERS - 1
        held = [None]

        def beside(k):
            if last:
                add_energy(k)
            elif k < 4:
                back(xs, k)
            else:
                if k == 4:
                    held[0] = stacked(y_ref[...])
                forth(held[0], k - 4)

        if last:
            fetch.wait()
        inverse = inverse_factor(gram_of(xs), beside)
        x = product(inverse, x if last else w_ref[...])
    hi, lo = split(x, 2)
    left_ref[...] = jnp.concatenate([hi, hi, lo, lo], 0)
    right_ref[...] = jnp.concatenate([hi, lo, hi, lo], 0)
    along = dot(hi, steer_ref[...], NN)
    energy = jnp.sum(energy_ref[...], axis=0, keepdims=True)
    noise = energy - jnp.sum(along * along, axis=0, keepdims=True)
    for c in range(G // 128):
        piece = noise[:, c * 128 : (c + 1) * 128]
        noise_ref[:, c, :] = jnp.broadcast_to(piece, (PLANE_SIZE, 128))


def subspace(data, steer, start):
    whole = pl.BlockSpec(memory_space=pltpu.VMEM)
    far = pl.BlockSpec(memory_space=pltpu.HBM)
    return pl.pallas_call(
        subspace_kernel,
        out_shape=(
            jax.ShapeDtypeStruct((PLANE_SIZE, G // 128, 128), jnp.float32),
            jax.ShapeDtypeStruct((4 * N, M), jnp.bfloat16),
            jax.ShapeDtypeStruct((4 * N, M), jnp.bfloat16),
        ),
        in_specs=[whole, far, whole],
        out_specs=(whole, whole, whole),
        scratch_shapes=[
            pltpu.VMEM((M, M), jnp.bfloat16),
            pltpu.VMEM((M, G), jnp.bfloat16),
            pltpu.VMEM((N, M), jnp.float32),
            pltpu.VMEM((N, M), jnp.float32),
            pltpu.VMEM((8, G), jnp.float32),
            pltpu.SemaphoreType.DMA,
        ],
        compiler_params=pltpu.CompilerParams(vmem_limit_bytes=52_000_000),
        name="subspace",
    )(data, steer, start)


def on_device(data, steering, start):
    owned = lax.all_to_all(data, AXES, split_axis=0, concat_axis=0, tiled=True)
    noise, left, right = subspace(owned, steering[0], start[0].T)
    total = lax.all_to_all(noise, PLANE, split_axis=0, concat_axis=0, tiled=True).sum(0)
    swap = [(0, 1), (1, 0)]
    one = lax.ppermute(total, "z0", swap)
    two = lax.ppermute(total, "z1", swap)
    three = lax.ppermute(total, ("z1", "z0"), [(z, 3 - z) for z in range(4)])
    total = (total + one) + (two + three)
    total = total + lax.ppermute(total, ("z2", "z1", "z0"), [(z, 7 - z) for z in range(8)])
    projector = lax.dot_general(
        left, right, (((0,), (0,)), ((), ())), preferred_element_type=jnp.float32
    )
    spectrum = F * M / total.reshape(G)
    return (projector[None], spectrum)


def solution(mesh):
    finer = Mesh(mesh.devices.reshape(4, 2, 2, 2, 2, 2, 2), AXES)
    by_bin = P(AXES, None, None)
    return jax.shard_map(
        on_device,
        mesh=finer,
        in_specs=(P(None, AXES, None), by_bin, by_bin),
        out_specs=(by_bin, P()),
        check_vma=False,
    )
```
